128 devices in a mesh: batch: 8 (over x, core), proto: 16 (over z, y).
Axes of the slice: x: 4, y: 4, z: 4, core: 2. Of those that a mesh axis runs over, the one named last changes fastest.
Arguments:
- teacher_feats: bfloat16 [16384, 256], P(('batch', 'proto')), may hold values from -20 to 20
- student_feats: bfloat16 [16384, 256], P(('batch', 'proto')), may hold values from -20 to 20
- teacher_protos: bfloat16 [65536, 256], P(('proto', 'batch')), may hold values from -9 to 9
- student_protos: bfloat16 [65536, 256], P(('proto', 'batch')), may hold values from -9 to 9
Outputs:
- feature_grad: float32 [16384, 256], P(('batch', 'proto'))
- proto_grad: float32 [65536, 256], P(('proto', 'batch'))
The draws below stay inside these ranges and needn't reach their ends.
All inputs are finite; a program needn't handle non-finite values.
Results may differ from the reference program's by a relative error of at most 0.0025.
Values may be sent and summed in bfloat16 or wider, within the bound.
No kernel may reach another device: no remote copies, remote signals or barrier semaphores. Data moves between devices by JAX's collectives and lax.ppermute only.
A program may use at most 192 MiB of HBM per device.

```python
import math
import jax
import jax.numpy as jnp
from jax import lax

DIM = 256
PROTOS = 65536
ITERS = 3
CROPS = 16384


def common_direction(key):
    return jnp.clip(jax.random.normal(jax.random.fold_in(key, 7), (DIM,), jnp.float32), -3.0, 3.0)


def anchor_rows(key):
    anchor = jnp.clip(jax.random.normal(jax.random.fold_in(key, 29), (PROTOS, DIM), jnp.float32), -3.0, 3.0)
    partner = jax.random.randint(jax.random.fold_in(key, 31), (CROPS,), 0, PROTOS)
    return (anchor, partner)


def feature_rows(noise, strength, direction):
    return (noise + strength * direction[None, :]).astype(jnp.bfloat16)


def rising(count, low, high):
    position = jnp.arange(count, dtype=jnp.float32)[:, None] / count
    return jnp.exp(jnp.log(low) + (jnp.log(high) - jnp.log(low)) * position)


def draw_teacher_feats(key, part):
    direction = common_direction(key)
    anchor, partner = anchor_rows(key)
    key = jax.random.fold_in(key, 11)
    noise_key, strength_key, pull_key = jax.random.split(key, 3)
    jitter = jnp.exp(jax.random.uniform(strength_key, (CROPS, 1), jnp.float32, -0.15, 0.15))
    noise = jnp.clip(jax.random.normal(noise_key, (CROPS, DIM), jnp.float32), -5.0, 5.0)
    strength = rising(CROPS, 0.1, 0.6) * jitter
    pull = jnp.exp(jax.random.uniform(pull_key, (CROPS, 1), jnp.float32, jnp.log(0.3), jnp.log(3.0)))
    return feature_rows(noise + pull * anchor[partner], strength, direction)


def draw_student_feats(key, part):
    direction = common_direction(key)
    key = jax.random.fold_in(key, 13)
    noise_key, strength_key = jax.random.split(key)
    noise = jnp.clip(jax.random.normal(noise_key, (CROPS, DIM), jnp.float32), -5.0, 5.0)
    strength = jnp.exp(jax.random.uniform(strength_key, (CROPS, 1), jnp.float32, jnp.log(0.3), jnp.log(3.0)))
    return feature_rows(noise, strength, direction)


def draw_teacher_protos(key, part):
    direction = common_direction(key)
    anchor, _ = anchor_rows(key)
    key = jax.random.fold_in(key, 17)
    noise_key, strength_key = jax.random.split(key)
    signed = jax.random.uniform(strength_key, (PROTOS, 1), jnp.float32, -1.0, 1.0)
    noise = jnp.clip(jax.random.normal(noise_key, (PROTOS, DIM), jnp.float32), -5.0, 5.0)
    strength = signed * rising(PROTOS, 0.2, 0.6)
    return feature_rows(anchor + 0.5 * noise, strength, direction)


def draw_student_protos(key, part):
    direction = common_direction(key)
    key = jax.random.fold_in(key, 19)
    noise_key, strength_key = jax.random.split(key)
    noise = jnp.clip(jax.random.normal(noise_key, (PROTOS, DIM), jnp.float32), -5.0, 5.0)
    strength = jax.random.uniform(strength_key, (PROTOS, 1), jnp.float32, -0.8, 0.8)
    return feature_rows(noise, strength, direction)


def setup_inputs(seed: int = 0) -> dict:
    seeds = jax.random.split(jax.random.key(seed), 5)
    return {
        "teacher_feats": draw_teacher_feats(jax.random.fold_in(seeds[4], 71), 0),
        "student_feats": draw_student_feats(jax.random.fold_in(seeds[4], 71), 0),
        "teacher_protos": draw_teacher_protos(jax.random.fold_in(seeds[4], 71), 0),
        "student_protos": draw_student_protos(jax.random.fold_in(seeds[4], 71), 0),
    }


teacher_temp = 0.07
student_temp = 0.1
epsilon = 1e-06

def normalize_rows(values):
    wide = values.astype(jnp.float32)
    scale = lax.rsqrt(lax.optimization_barrier(jnp.sum(wide * wide, -1, keepdims=True)) + epsilon)
    return (wide * scale, scale)

def rounded(values):
    return lax.optimization_barrier(values.astype(jnp.bfloat16)).astype(jnp.float32)

def project_back(grad, unit_rows, scale):
    return (grad - unit_rows * lax.optimization_barrier(jnp.sum(unit_rows * grad, -1, keepdims=True))) * scale

def reference(teacher_feats, student_feats, teacher_protos, student_protos):
    teacher_unit, _ = normalize_rows(teacher_feats)
    student_unit, student_scale = normalize_rows(student_feats)
    tproto_unit, _ = normalize_rows(teacher_protos)
    sproto_unit, sproto_scale = normalize_rows(student_protos)
    teacher_round = rounded(teacher_unit)
    student_round = rounded(student_unit)
    tproto_round = rounded(tproto_unit)
    sproto_round = rounded(sproto_unit)
    block_size = math.gcd(CROPS, 1024)
    block_count = CROPS // block_size
    teacher_blocks = teacher_round.reshape(block_count, block_size, DIM)
    student_blocks = student_round.reshape(block_count, block_size, DIM)
    contract_last = (((1,), (1,)), ((), ()))

    def teacher_exp(rows_block):
        logits = lax.dot_general(rows_block, tproto_round, contract_last, precision=lax.Precision.HIGHEST)
        return jnp.exp(logits / teacher_temp)
    crop_weight = jnp.ones((CROPS,), jnp.float32)
    proto_weight = jnp.ones((PROTOS,), jnp.float32)
    for iteration in range(ITERS):

        def add_column(running, pair_item):
            rows_block, block_weight = pair_item
            return (running + jnp.dot(block_weight, teacher_exp(rows_block), precision=lax.Precision.HIGHEST), None)
        column_total, _ = lax.scan(add_column, jnp.zeros((PROTOS,), jnp.float32), (teacher_blocks, crop_weight.reshape(block_count, block_size)))
        proto_weight = 1.0 / column_total

        def row_total(rows_block, weights=proto_weight):
            return jnp.dot(teacher_exp(rows_block), weights, precision=lax.Precision.HIGHEST)
        crop_weight = 1.0 / lax.map(row_total, teacher_blocks).reshape(CROPS)

    def grad_block(running, triple):
        teacher_block, student_block, block_weight = triple
        logits = lax.dot_general(student_block, sproto_round, contract_last, precision=lax.Precision.HIGHEST) / student_temp
        expo = jnp.exp(logits)
        probs = expo / lax.optimization_barrier(jnp.sum(expo, 1, keepdims=True))
        targets = block_weight[:, None] * (teacher_exp(teacher_block) * proto_weight[None, :])
        logit_grad = rounded((probs - targets) / student_temp)
        feature_block = jnp.dot(logit_grad, sproto_round, precision=lax.Precision.HIGHEST)
        proto_part = lax.dot_general(logit_grad, student_block, (((0,), (0,)), ((), ())), precision=lax.Precision.HIGHEST)
        return (running + proto_part, feature_block)
    proto_total, feature_blocks = lax.scan(grad_block, jnp.zeros((PROTOS, DIM), jnp.float32), (teacher_blocks, student_blocks, crop_weight.reshape(block_count, block_size)))
    feature_total = feature_blocks.reshape(CROPS, DIM)
    feature_grad = project_back(feature_total, student_unit, student_scale)
    proto_grad = project_back(proto_total, sproto_unit, sproto_scale)
    return (feature_grad, proto_grad)
```

```python
import functools

import jax
import jax.numpy as jnp
from jax import lax
from jax.experimental import pallas as pl
from jax.experimental.pallas import tpu as pltpu
from jax.sharding import PartitionSpec as P

ITERS = 3
LOG2E = 1.4426950408889634
teacher_temp = 0.07
student_temp = 0.1
epsilon = 1e-06

F32 = jnp.float32
BF16 = jnp.bfloat16
MIB = 2**20
VM = pl.BlockSpec(memory_space=pltpu.VMEM)
SM = pl.BlockSpec(memory_space=pltpu.SMEM)
NT = (((1,), (1,)), ((), ()))
NN = (((1,), (0,)), ((), ()))
TN = (((0,), (0,)), ((), ()))


def normalize_rows(values):
    wide = values.astype(F32)
    scale = lax.rsqrt(jnp.sum(wide * wide, -1, keepdims=True) + epsilon)
    return (wide * scale, scale)


def project_back(grad, unit_rows, scale):
    return (grad - unit_rows * jnp.sum(unit_rows * grad, -1, keepdims=True)) * scale


def fold(x):
    return x.reshape(-1, 8, x.shape[1]).sum(0)


def spread(row, out):
    for k in range(row.shape[1] // 128):
        part = row[:, k * 128 : (k + 1) * 128]
        out[k * 128 : (k + 1) * 128, :] = jnp.broadcast_to(part, (128, 128)).T


def gather_lanes(part, out):
    for k in range(part.shape[0] // 128):
        out[:, k * 128 : (k + 1) * 128] = part[k * 128 : (k + 1) * 128, :].T.sum(0, keepdims=True)


def exp_kernel(dim, me, feats, *refs):
    pieces, (e, c, protos, own_protos) = refs[:-4], refs[-4:]
    own = pieces[0].shape[0]
    for r, piece in enumerate(pieces):
        own_protos[r] = piece[:, :dim]
        protos[r] = piece[:, dim:]

    @pl.loop(0, len(pieces))
    def _(r):
        s = lax.dot_general(feats[:, :dim], own_protos[r], NT, preferred_element_type=F32)
        x = jnp.exp2(s * (LOG2E / teacher_temp))
        e[:, pl.ds(pl.multiple_of(r * own, own), own)] = x
        c[:, pl.ds(pl.multiple_of((me[0] ^ r) * own, own), own)] = fold(x).sum(0, keepdims=True)


def total_kernel(dim, feats, protos, z, part):
    own = protos.shape[1]
    part[...] = jnp.zeros_like(part)

    @pl.loop(0, protos.shape[0])
    def _(r):
        s = lax.dot_general(feats[:, dim:], protos[r], NT, preferred_element_type=F32)
        x = jnp.exp2(s * (LOG2E / student_temp))
        acc = x[:, :128]
        for k in range(1, own // 128):
            acc += x[:, k * 128 : (k + 1) * 128]
        part[...] += acc

    gather_lanes(part, z)


def row_kernel(block, own, me, e, c0, c1, c2, c3, r, b, part):
    rows, cols = e.shape
    for k in range(cols // own):
        src = pl.ds(pl.multiple_of((me[0] ^ k) * own, own), own)
        b[:, k * own : (k + 1) * own] = 1.0 / (c0[:, src] + c1[:, src] + c2[:, src] + c3[:, src])

    @pl.loop(0, rows // block)
    def _(i):
        ii = pl.ds(pl.multiple_of(i * block, block), block)
        acc = jnp.zeros((block, 128), F32)
        for k in range(cols // 128):
            lanes = slice(k * 128, (k + 1) * 128)
            acc += e[ii, lanes] * b[:, lanes]
        part[ii, :] = acc

    gather_lanes(part, r)


def col_kernel(block, width, own, me, e, sums, c, av):
    rows, cols = e.shape
    spread(1.0 / jnp.sum(sums[...], 0, keepdims=True), av)
    for j in range(cols // width):

        def step(i, acc, j=j):
            ii = pl.ds(pl.multiple_of(i * block, block), block)
            w = av[ii, :]
            return tuple(
                acc[k] + fold(e[ii, j * width + k * 128 : j * width + (k + 1) * 128] * w)
                for k in range(width // 128)
            )

        zero = jnp.zeros((8, 128), F32)
        acc = lax.fori_loop(0, rows // block, step, (zero,) * (width // 128))
        for k in range(width // own):
            part = jnp.concatenate(acc[k * own // 128 : (k + 1) * own // 128], 1)
            to = (me[0] ^ (j * width // own + k)) * own
            c[:, pl.ds(pl.multiple_of(to, own), own)] = part.sum(0, keepdims=True)


def grad_kernel(dim, me, e, feats, b, sums, zsums, protos, f_out, keep, give, av, zv, g0, g1, f_acc):
    own = protos.shape[1]
    spread((1.0 / student_temp) / jnp.sum(sums[...], 0, keepdims=True), av)
    spread((1.0 / student_temp) / jnp.sum(zsums[...], 0, keepdims=True), zv)
    f_acc[...] = jnp.zeros_like(f_acc)
    wide = lambda m: jnp.concatenate([m] * (own // 128), 1)

    @pl.loop(0, protos.shape[0] // 2)
    def _(h):
        for k, (g, out) in enumerate(((g0, keep), (g1, give))):
            cols = pl.ds(pl.multiple_of((2 * h + k) * own, own), own)
            sp = protos[2 * h + k]
            s = lax.dot_general(feats[:, dim:], sp, NT, preferred_element_type=F32)
            p = jnp.exp2(s * (LOG2E / student_temp))
            g[...] = (p * wide(zv[...]) - wide(av[...]) * (e[:, cols] * b[:, cols])).astype(BF16)
            out[h] = lax.dot_general(g[...], feats[:, dim:], TN, preferred_element_type=F32)
            f_acc[...] += lax.dot_general(g[...], sp, NN, preferred_element_type=F32)
    f_out[...] = f_acc[...].astype(BF16).reshape(f_out.shape)


def call(kernel, name, out_shape, ops, scratch=(), limit=22, smem=0):
    many = isinstance(out_shape, (list, tuple))
    return pl.pallas_call(
        kernel,
        out_shape=out_shape,
        in_specs=[SM] * smem + [VM] * (len(ops) - smem),
        out_specs=[VM] * len(out_shape) if many else VM,
        scratch_shapes=list(scratch),
        compiler_params=pltpu.CompilerParams(vmem_limit_bytes=limit * MIB),
        name=name,
    )(*ops)


def shards(nb, npr, teacher_feats, student_feats, teacher_protos, student_protos):
    sds = jax.ShapeDtypeStruct
    swap = lambda x, k: lax.ppermute(x, "batch", [(i, i ^ k) for i in range(nb)])

    def over_proto(x):
        return lax.all_to_all(jnp.broadcast_to(x[None], (npr,) + x.shape), "proto", 0, 0)

    dim = teacher_feats.shape[1]
    own_rows, own = student_feats.shape[0], student_protos.shape[0]
    rows, cols = own_rows * npr, own * nb
    me = lax.axis_index("batch").astype(jnp.int32).reshape(1)
    teacher_unit, _ = normalize_rows(teacher_feats)
    student_unit, student_scale = normalize_rows(student_feats)
    tproto_unit, _ = normalize_rows(teacher_protos)
    sproto_unit, sproto_scale = normalize_rows(student_protos)
    mine = jnp.concatenate([tproto_unit, sproto_unit], 1).astype(BF16)
    pieces = [None] * nb
    pieces[0] = mine
    for r in range(2, nb, 2):
        pieces[r] = swap(mine, r)
    feats = over_proto(jnp.concatenate([teacher_unit, student_unit], 1).astype(BF16))
    feats = feats.reshape(rows, 2 * dim)
    for r in range(0, nb, 2):
        pieces[r + 1] = swap(pieces[r], 1)

    e, c, protos = call(
        functools.partial(exp_kernel, dim),
        "teacher_exp",
        [pltpu.VMEM((rows, cols), F32), sds((1, cols), F32), pltpu.VMEM((nb, own, dim), BF16)],
        [me, feats, *pieces],
        [pltpu.VMEM((nb, own, dim), BF16)],
        smem=1,
    )
    e = pltpu.with_memory_space_constraint(e, pltpu.VMEM)
    protos = pltpu.with_memory_space_constraint(protos, pltpu.VMEM)
    lanes = pltpu.VMEM((rows, 128), F32)
    z = call(
        functools.partial(total_kernel, dim),
        "student_total",
        sds((1, rows), F32),
        [feats, protos],
        [lanes],
    )
    for iteration in range(ITERS):
        if iteration:
            c = call(
                functools.partial(col_kernel, 128, 2048, own),
                "column_sums",
                sds((1, cols), F32),
                [me, e, sums],
                [lanes],
                smem=1,
            )
        c = c + swap(c, 1)
        cs = [c] + [swap(c, k) for k in range(2, nb, 2)]
        r, b = call(
            functools.partial(row_kernel, 128, own),
            "row_sums",
            [sds((1, rows), F32), sds((1, cols), F32)],
            [me, e, *cs],
            [lanes],
            smem=1,
        )
        if iteration == 0:
            both = over_proto(jnp.concatenate([r, z], 0))
            sums, zsums = both[:, 0], both[:, 1]
        else:
            sums = over_proto(r).reshape(npr, rows)
    half_g = pltpu.VMEM((rows, own), BF16)
    f, keep, give = call(
        functools.partial(grad_kernel, dim),
        "logit_grad",
        [
            sds((npr, own_rows, dim), BF16),
            sds((nb // 2, own, dim), F32),
            sds((nb // 2, own, dim), F32),
        ],
        [me, e, feats, b, sums, zsums, protos],
        [lanes, lanes, half_g, half_g, pltpu.VMEM((rows, dim), F32)],
        smem=1,
    )
    half = keep + swap(give, 1)
    sent = [swap(half[k].astype(BF16), 2 * k) for k in range(1, nb // 2)]
    f = lax.all_to_all(f, "proto", 0, 0)
    feature_part = jnp.sum(f.astype(F32), 0)
    proto_part = half[0] + sum(x.astype(F32) for x in sent)
    feature_grad = project_back(feature_part, student_unit, student_scale)
    proto_grad = project_back(proto_part, sproto_unit, sproto_scale)
    return (feature_grad, proto_grad)


def solution(mesh):
    nb, npr = mesh.shape["batch"], mesh.shape["proto"]
    in_specs = (
        P(("batch", "proto"), None),
        P(("batch", "proto"), None),
        P(("proto", "batch"), None),
        P(("proto", "batch"), None),
    )
    out_specs = (P(("batch", "proto"), None), P(("proto", "batch"), None))
    return jax.shard_map(
        functools.partial(shards, nb, npr),
        mesh=mesh,
        in_specs=in_specs,
        out_specs=out_specs,
        check_vma=False,
    )
```

```python
import functools

import jax
import jax.numpy as jnp
from jax import lax
from jax.experimental import pallas as pl
from jax.experimental.pallas import tpu as pltpu
from jax.sharding import PartitionSpec as P

ITERS = 3
LOG2E = 1.4426950408889634
teacher_temp = 0.07
student_temp = 0.1
epsilon = 1e-06

F32 = jnp.float32
BF16 = jnp.bfloat16
MIB = 2**20
VM = pl.BlockSpec(memory_space=pltpu.VMEM)
SM = pl.BlockSpec(memory_space=pltpu.SMEM)
NT = (((1,), (1,)), ((), ()))
NN = (((1,), (0,)), ((), ()))


def project_back(grad, unit_rows, scale):
    return (grad - unit_rows * jnp.sum(unit_rows * grad, -1, keepdims=True)) * scale


def fold(x):
    return x.reshape(-1, 8, x.shape[1]).sum(0)


def spread(row, out):
    for k in range(row.shape[1] // 128):
        part = row[:, k * 128 : (k + 1) * 128]
        out[k * 128 : (k + 1) * 128, :] = jnp.broadcast_to(part, (128, 128)).T


def gather_lanes(part, out):
    for k in range(part.shape[0] // 128):
        out[0:1, k * 128 : (k + 1) * 128] = part[k * 128 : (k + 1) * 128, :].T.sum(0, keepdims=True)


def unit_kernel(tf, sf, tp, sp, feats, protos, fscale, pscale):
    dim = tf.shape[1]
    for k, (x, y) in enumerate(((tf, tp), (sf, sp))):
        half = slice(k * dim, (k + 1) * dim)
        wide = x[...].astype(F32)
        scale = lax.rsqrt(jnp.sum(wide * wide, -1, keepdims=True) + epsilon)
        unit = (wide * scale).astype(BF16)
        for i in range(feats.shape[0]):
            feats[i, :, half] = unit
        if k:
            fscale[...] = scale
        wide = y[...].astype(F32)
        scale = lax.rsqrt(jnp.sum(wide * wide, -1, keepdims=True) + epsilon)
        protos[:, half] = (wide * scale).astype(BF16)
        if k:
            pscale[...] = scale


def exp_kernel(dim, me, feats, *refs):
    pieces, (e, c, protos) = refs[:-3], refs[-3:]
    own = pieces[0].shape[0]
    for r, piece in enumerate(pieces):
        protos[r] = piece[:, :dim]

    @pl.loop(0, len(pieces))
    def _(r):
        s = lax.dot_general(feats[:, :dim], protos[r], NT, preferred_element_type=F32)
        x = jnp.exp2(s * (LOG2E / teacher_temp))
        e[:, pl.ds(pl.multiple_of(r * own, own), own)] = x
        c[:, pl.ds(pl.multiple_of((me[0] ^ r) * own, own), own)] = fold(x).sum(0, keepdims=True)


def total_kernel(dim, feats, *refs):
    pieces, (z, protos, part) = refs[:-3], refs[-3:]
    own = pieces[0].shape[0]
    for r, piece in enumerate(pieces):
        protos[r] = piece[:, dim:]
    part[...] = jnp.zeros_like(part)

    @pl.loop(0, len(pieces))
    def _(r):
        s = lax.dot_general(feats[:, dim:], protos[r], NT, preferred_element_type=F32)
        x = jnp.exp2(s * (LOG2E / student_temp))
        acc = x[:, :128]
        for k in range(1, own // 128):
            acc += x[:, k * 128 : (k + 1) * 128]
        part[...] += acc

    gather_lanes(part, z)


def row_kernel(block, own, me, e, c0, c1, c2, c3, *refs):
    z, (r, b, part) = refs[:-3], refs[-3:]
    rows, cols = e.shape
    for k in range(cols // own):
        src = pl.ds(pl.multiple_of((me[0] ^ k) * own, own), own)
        b[:, k * own : (k + 1) * own] = 1.0 / (c0[:, src] + c1[:, src] + c2[:, src] + c3[:, src])

    @pl.loop(0, rows // block)
    def _(i):
        ii = pl.ds(pl.multiple_of(i * block, block), block)
        acc = jnp.zeros((block, 128), F32)
        for k in range(cols // 128):
            lanes = slice(k * 128, (k + 1) * 128)
            acc += e[ii, lanes] * b[:, lanes]
        part[ii, :] = acc

    gather_lanes(part, r.at[0])
    for k in range(len(z)):
        r[0, k + 1 : k + 2, :] = z[k][...]
    for k in range(1, r.shape[0]):
        r[k] = r[0]


def col_kernel(block, width, own, me, e, sums, c, av):
    rows, cols = e.shape
    spread(1.0 / jnp.sum(sums[:, 0, :], 0, keepdims=True), av)
    for j in range(cols // width):

        def step(i, acc, j=j):
            ii = pl.ds(pl.multiple_of(i * block, block), block)
            w = av[ii, :]
            return tuple(
                acc[k] + fold(e[ii, j * width + k * 128 : j * width + (k + 1) * 128] * w)
                for k in range(width // 128)
            )

        zero = jnp.zeros((8, 128), F32)
        acc = lax.fori_loop(0, rows // block, step, (zero,) * (width // 128))
        for k in range(width // own):
            part = jnp.concatenate(acc[k * own // 128 : (k + 1) * own // 128], 1)
            to = (me[0] ^ (j * width // own + k)) * own
            c[:, pl.ds(pl.multiple_of(to, own), own)] = part.sum(0, keepdims=True)


def grad_kernel(dim, me, e, feats, b, protos, sums, zsums, f, keep, give, av, zv, g0, g1, acc, turned):
    own = protos.shape[1]
    spread((1.0 / student_temp) / jnp.sum(sums[:, 0, :], 0, keepdims=True), av)
    spread((1.0 / student_temp) / jnp.sum(zsums[:, 1, :], 0, keepdims=True), zv)
    acc[...] = jnp.zeros_like(acc)
    turned[...] = feats[:, dim:].T
    wide = lambda m: jnp.concatenate([m] * (own // 128), 1)

    @pl.loop(0, protos.shape[0] // 2)
    def _(h):
        for k, (g, out) in enumerate(((g0, keep), (g1, give))):
            cols = pl.ds(pl.multiple_of((2 * h + k) * own, own), own)
            sp = protos[2 * h + k]
            s = lax.dot_general(feats[:, dim:], sp, NT, preferred_element_type=F32)
            p = jnp.exp2(s * (LOG2E / student_temp))
            g[...] = (p * wide(zv[...]) - wide(av[...]) * (e[:, cols] * b[:, cols])).astype(BF16)
            new = lax.dot_general(turned[...], g[...], NN, preferred_element_type=F32)
            out[h] = new.T.astype(out.dtype)
            acc[...] += lax.dot_general(g[...], sp, NN, preferred_element_type=F32)

    f[...] = acc[...].astype(BF16).reshape(f.shape)


def call(kernel, name, out_shape, ops, scratch=(), limit=26, smem=0, keep=()):
    many = isinstance(out_shape, (list, tuple))
    ops = list(ops[:smem]) + [
        pltpu.with_memory_space_constraint(x, pltpu.VMEM if i in keep else pltpu.HBM)
        for i, x in enumerate(ops[smem:])
    ]
    return pl.pallas_call(
        kernel,
        out_shape=out_shape,
        in_specs=[SM] * smem + [VM] * (len(ops) - smem),
        out_specs=[VM] * len(out_shape) if many else VM,
        scratch_shapes=list(scratch),
        compiler_params=pltpu.CompilerParams(vmem_limit_bytes=limit * MIB),
        name=name,
    )(*ops)


def shards(nb, npr, teacher_feats, student_feats, teacher_protos, student_protos):
    swap = lambda x, k: lax.ppermute(x, "batch", [(i, i ^ k) for i in range(nb)])

    dim = teacher_feats.shape[1]
    own_rows, own = student_feats.shape[0], student_protos.shape[0]
    rows, cols = own_rows * npr, own * nb
    me = lax.axis_index("batch").astype(jnp.int32).reshape(1)
    hbm, vmem = pltpu.HBM, pltpu.VMEM

    feats, unit, fscale, pscale = call(
        unit_kernel,
        "unit_rows",
        [
            hbm((npr, own_rows, 2 * dim), BF16),
            hbm((own, 2 * dim), BF16),
            hbm((own_rows, 1), F32),
            hbm((own, 1), F32),
        ],
        [teacher_feats, student_feats, teacher_protos, student_protos],
    )
    pieces = [unit] + [None] * (nb - 1)
    for r in range(2, nb, 2):
        pieces[r] = swap(unit, r)
    feats = lax.all_to_all(feats, "proto", 0, 0).reshape(rows, 2 * dim)
    for r in range(0, nb, 2):
        pieces[r + 1] = swap(pieces[r], 1)

    lanes = vmem((rows, 128), F32)
    all_cols = vmem((1, cols), F32)
    e, c = call(
        functools.partial(exp_kernel, dim),
        "teacher_exp",
        [vmem((rows, cols), F32), all_cols],
        [me, feats, *pieces],
        [vmem((nb, own, dim), BF16)],
        smem=1,
    )
    for iteration in range(ITERS):
        if iteration:
            c = call(
                functools.partial(col_kernel, 128, 2048, own),
                "column_sums",
                all_cols,
                [me, e, sums],
                [lanes],
                smem=1,
                keep=(0,),
            )
        c = c + swap(c, 1)
        cs = [c] + [swap(c, k) for k in range(2, nb, 2)]
        extra = [z] if iteration == 1 else []
        r, b = call(
            functools.partial(row_kernel, 128, own),
            "row_sums",
            [hbm((npr, 1 + len(extra), rows), F32), all_cols],
            [me, e, *cs, *extra],
            [lanes],
            smem=1,
            keep=(0, 1, 2, 3, 4),
        )
        if iteration == 0:
            r, feats_z = lax.optimization_barrier((r, feats))
            z, protos = call(
                functools.partial(total_kernel, dim),
                "student_total",
                [hbm((1, rows), F32), hbm((nb, own, dim), BF16)],
                [feats_z, *pieces],
                [lanes],
            )
        sums = lax.all_to_all(r, "proto", 0, 0)
        if extra:
            zsums = sums
    half_g = vmem((rows, own), BF16)
    f, keep, give = call(
        functools.partial(grad_kernel, dim),
        "logit_grad",
        [
            hbm((npr, own_rows, dim), BF16),
            hbm((nb // 2, own, dim), F32),
            hbm((nb // 2, own, dim), BF16),
        ],
        [me, e, feats, b, protos, sums, zsums],
        [lanes, lanes, half_g, half_g, vmem((rows, dim), F32), vmem((dim, rows), BF16)],
        smem=1,
        keep=(0, 2),
    )
    half = keep + swap(give, 1).astype(F32)
    sent = [swap(half[k].astype(BF16), 2 * k) for k in range(1, nb // 2)]
    f, *sent = lax.optimization_barrier((lax.all_to_all(f, "proto", 0, 0), *sent))
    feature_part = jnp.sum(f.astype(F32), 0)
    proto_part = half[0] + sum(x.astype(F32) for x in sent)
    student_unit = student_feats.astype(F32) * fscale
    sproto_unit = student_protos.astype(F32) * pscale
    feature_grad = project_back(feature_part, student_unit, fscale)
    proto_grad = project_back(proto_part, sproto_unit, pscale)
    return (feature_grad, proto_grad)


def solution(mesh):
    nb, npr = mesh.shape["batch"], mesh.shape["proto"]
    in_specs = (
        P(("batch", "proto"), None),
        P(("batch", "proto"), None),
        P(("proto", "batch"), None),
        P(("proto", "batch"), None),
    )
    out_specs = (P(("batch", "proto"), None), P(("proto", "batch"), None))
    return jax.shard_map(
        functools.partial(shards, nb, npr),
        mesh=mesh,
        in_specs=in_specs,
        out_specs=out_specs,
        check_vma=False,
    )
```

```python
import functools

import jax
import jax.numpy as jnp
from jax import lax
from jax.experimental import pallas as pl
from jax.experimental.pallas import tpu as pltpu
from jax.sharding import PartitionSpec as P

ITERS = 3
LOG2E = 1.4426950408889634
teacher_temp = 0.07
student_temp = 0.1
epsilon = 1e-06

F32 = jnp.float32
BF16 = jnp.bfloat16
MIB = 2**20
VM = pl.BlockSpec(memory_space=pltpu.VMEM)
SM = pl.BlockSpec(memory_space=pltpu.SMEM)
NT = (((1,), (1,)), ((), ()))
NN = (((1,), (0,)), ((), ()))


def unit_rows(x):
    wide = x.astype(F32)
    scale = lax.rsqrt(jnp.sum(wide * wide, -1, keepdims=True) + epsilon)
    return (wide * scale, scale)


def project_back(grad, x):
    unit, scale = unit_rows(x)
    return (grad - unit * jnp.sum(unit * grad, -1, keepdims=True)) * scale


def fold(x):
    return x.reshape(-1, 8, x.shape[1]).sum(0)


def spread(row, out):
    for k in range(row.shape[1] // 128):
        part = row[:, k * 128 : (k + 1) * 128]
        out[k * 128 : (k + 1) * 128, :] = jnp.broadcast_to(part, (128, 128)).T


def gather_lanes(part, out):
    for k in range(part.shape[0] // 128):
        out[0:1, k * 128 : (k + 1) * 128] = part[k * 128 : (k + 1) * 128, :].T.sum(0, keepdims=True)


def unit_kernel(tf, sf, tp, sp, feats, protos):
    dim = tf.shape[1]
    for k, (x, y) in enumerate(((tf, tp), (sf, sp))):
        half = slice(k * dim, (k + 1) * dim)
        unit = unit_rows(x[...])[0].astype(BF16)
        for i in range(feats.shape[0]):
            feats[i, :, half] = unit
        protos[:, half] = unit_rows(y[...])[0].astype(BF16)


def load_half(half, feats, pieces, ft, pt, sem):
    dim = ft.shape[1]
    cols = pl.ds(half * dim, dim)
    first = pltpu.make_async_copy(feats.at[:, cols], ft, sem.at[len(pieces)])
    first.start()
    for r, piece in enumerate(pieces):
        pltpu.make_async_copy(piece.at[:, cols], pt.at[r], sem.at[r]).start()

    def wait_piece(r):
        pltpu.make_async_copy(pieces[0].at[:, cols], pt.at[r], sem.at[r]).wait()

    return first.wait, wait_piece


def exp_kernel(me, feats, *refs):
    pieces, (e, c, ft, pt, sem) = refs[:-5], refs[-5:]
    own = pt.shape[1]
    wait_feats, wait_piece = load_half(0, feats, pieces, ft, pt, sem)
    wait_feats()

    @pl.loop(0, len(pieces))
    def _(r):
        wait_piece(r)
        s = lax.dot_general(ft[...], pt[r], NT, preferred_element_type=F32)
        x = jnp.exp2(s * (LOG2E / teacher_temp))
        e[:, pl.ds(pl.multiple_of(r * own, own), own)] = x
        c[:, pl.ds(pl.multiple_of((me[0] ^ r) * own, own), own)] = fold(x).sum(0, keepdims=True)


def total_kernel(feats, *refs):
    pieces, (z, ft, pt, sem, part) = refs[:-5], refs[-5:]
    own = pt.shape[1]
    wait_feats, wait_piece = load_half(1, feats, pieces, ft, pt, sem)
    part[...] = jnp.zeros_like(part)
    wait_feats()

    @pl.loop(0, len(pieces))
    def _(r):
        wait_piece(r)
        s = lax.dot_general(ft[...], pt[r], NT, preferred_element_type=F32)
        x = jnp.exp2(s * (LOG2E / student_temp))
        acc = x[:, :128]
        for k in range(1, own // 128):
            acc += x[:, k * 128 : (k + 1) * 128]
        part[...] += acc

    gather_lanes(part, z)


def row_kernel(block, own, me, e, c0, c1, c2, c3, *refs):
    z, (r, b, part) = refs[:-3], refs[-3:]
    rows, cols = e.shape
    for k in range(cols // own):
        src = pl.ds(pl.multiple_of((me[0] ^ k) * own, own), own)
        b[:, k * own : (k + 1) * own] = 1.0 / (c0[:, src] + c1[:, src] + c2[:, src] + c3[:, src])

    @pl.loop(0, rows // block)
    def _(i):
        ii = pl.ds(pl.multiple_of(i * block, block), block)
        acc = jnp.zeros((block, 128), F32)
        for k in range(cols // 128):
            lanes = slice(k * 128, (k + 1) * 128)
            acc += e[ii, lanes] * b[:, lanes]
        part[ii, :] = acc

    gather_lanes(part, r.at[0])
    if z:
        r[0, 1:2, :] = z[0][...]
    for k in range(1, r.shape[0]):
        r[k] = r[0]


def col_kernel(block, width, own, me, e, sums, c, av):
    rows, cols = e.shape
    spread(1.0 / jnp.sum(sums[:, 0, :], 0, keepdims=True), av)
    for j in range(cols // width):

        def step(i, acc, j=j):
            ii = pl.ds(pl.multiple_of(i * block, block), block)
            w = av[ii, :]
            return tuple(
                acc[k] + fold(e[ii, j * width + k * 128 : j * width + (k + 1) * 128] * w)
                for k in range(width // 128)
            )

        zero = jnp.zeros((8, 128), F32)
        acc = lax.fori_loop(0, rows // block, step, (zero,) * (width // 128))
        for k in range(width // own):
            part = jnp.concatenate(acc[k * own // 128 : (k + 1) * own // 128], 1)
            to = (me[0] ^ (j * width // own + k)) * own
            c[:, pl.ds(pl.multiple_of(to, own), own)] = part.sum(0, keepdims=True)


def grad_kernel(count, e, feats, b, sums, zsums, *refs):
    pieces, refs = refs[:count], refs[count:]
    f, keep, give, ft, pt, sem, av, zv, g0, g1, acc, turned, kept, given, out_sem = refs
    own = pt.shape[1]
    wait_feats, wait_piece = load_half(1, feats, pieces, ft, pt, sem)
    spread((1.0 / student_temp) / jnp.sum(sums[:, 0, :], 0, keepdims=True), av)
    spread((1.0 / student_temp) / jnp.sum(zsums[:, 1, :], 0, keepdims=True), zv)
    acc[...] = jnp.zeros_like(acc)
    wait_feats()
    turned[...] = ft[...].T
    wide = lambda m: jnp.concatenate([m] * (own // 128), 1)

    def put(h, k):
        src, dst = ((kept, keep), (given, give))[k]
        return pltpu.make_async_copy(src.at[h], dst.at[h], out_sem.at[h, k])

    @pl.loop(0, count // 2)
    def _(h):
        new = []
        wait_piece(2 * h)
        wait_piece(2 * h + 1)
        for k, (g, out) in enumerate(((g0, kept), (g1, given))):
            cols = pl.ds(pl.multiple_of((2 * h + k) * own, own), own)
            sp = pt[2 * h + k]
            s = lax.dot_general(ft[...], sp, NT, preferred_element_type=F32)
            p = jnp.exp2(s * (LOG2E / student_temp))
            g[...] = (p * wide(zv[...]) - wide(av[...]) * (e[:, cols] * b[:, cols])).astype(BF16)
            out[h] = lax.dot_general(turned[...], g[...], NN, preferred_element_type=F32).T.astype(out.dtype)
            new.append(lax.dot_general(g[...], sp, NN, preferred_element_type=F32))
        acc[...] += new[0] + new[1]
        put(h, 0).start()
        put(h, 1).start()

    f[...] = acc[...].astype(BF16).reshape(f.shape)
    for h in range(count // 2):
        put(h, 0).wait()
        put(h, 1).wait()


def merge_kernel(keep, got, first, *rest):
    first[...] = keep[0] + got[0].astype(F32)
    for k, out in enumerate(rest):
        out[...] = (keep[k + 1] + got[k + 1].astype(F32)).astype(BF16)


def final_kernel(f, sf, sp, half, *refs):
    got, (f_out, p_out) = refs[:-2], refs[-2:]
    f_out[...] = project_back(jnp.sum(f[...].astype(F32), 0), sf[...])
    p = half[...]
    for x in got:
        p += x[...].astype(F32)
    p_out[...] = project_back(p, sp[...])


def call(kernel, name, out_shape, ops, scratch=(), limit=26, smem=0, keep=(), raw=(), raw_out=()):
    many = isinstance(out_shape, (list, tuple))
    ops = list(ops[:smem]) + [
        pltpu.with_memory_space_constraint(x, pltpu.VMEM if i in keep else pltpu.HBM)
        for i, x in enumerate(ops[smem:])
    ]
    whole = pl.BlockSpec(memory_space=pl.ANY)
    return pl.pallas_call(
        kernel,
        out_shape=out_shape,
        in_specs=[SM] * smem + [whole if i in raw else VM for i in range(len(ops) - smem)],
        out_specs=[whole if i in raw_out else VM for i in range(len(out_shape))] if many else VM,
        scratch_shapes=list(scratch),
        compiler_params=pltpu.CompilerParams(vmem_limit_bytes=limit * MIB),
        name=name,
    )(*ops)


def shards(nb, npr, teacher_feats, student_feats, teacher_protos, student_protos):
    swap = lambda x, k: lax.ppermute(x, "batch", [(i, i ^ k) for i in range(nb)])

    dim = teacher_feats.shape[1]
    own_rows, own = student_feats.shape[0], student_protos.shape[0]
    rows, cols = own_rows * npr, own * nb
    me = lax.axis_index("batch").astype(jnp.int32).reshape(1)
    hbm, vmem = pltpu.HBM, pltpu.VMEM

    feats, unit = call(
        unit_kernel,
        "unit_rows",
        [hbm((npr, own_rows, 2 * dim), BF16), hbm((own, 2 * dim), BF16)],
        [teacher_feats, student_feats, teacher_protos, student_protos],
    )
    pieces = [unit] + [None] * (nb - 1)
    for r in range(2, nb, 2):
        pieces[r] = swap(unit, r)
    feats = lax.all_to_all(feats, "proto", 0, 0).reshape(rows, 2 * dim)
    for r in range(0, nb, 2):
        pieces[r + 1] = swap(pieces[r], 1)

    lanes = vmem((rows, 128), F32)
    all_cols = vmem((1, cols), F32)
    halves = [vmem((rows, dim), BF16), vmem((nb, own, dim), BF16), pltpu.SemaphoreType.DMA((nb + 1,))]
    e, c = call(
        exp_kernel,
        "teacher_exp",
        [vmem((rows, cols), F32), all_cols],
        [me, feats, *pieces],
        halves,
        smem=1,
        raw=range(nb + 1),
    )
    for iteration in range(ITERS):
        if iteration:
            c = call(
                functools.partial(col_kernel, 128, 2048, own),
                "column_sums",
                all_cols,
                [me, e, sums],
                [lanes],
                smem=1,
                keep=(0, 1),
            )
        c = c + swap(c, 1)
        cs = [c] + [swap(c, k) for k in range(2, nb, 2)]
        if iteration == 1:
            z = call(
                total_kernel,
                "student_total",
                hbm((1, rows), F32),
                [feats, *pieces],
                halves + [lanes],
                raw=range(nb + 1),
            )
        extra = [z] if iteration == 1 else []
        r, b = call(
            functools.partial(row_kernel, 128, own),
            "row_sums",
            [vmem((npr, 1 + len(extra), rows), F32), all_cols],
            [me, e, *cs, *extra],
            [lanes],
            smem=1,
            keep=(0, 1, 2, 3, 4),
        )
        sums = lax.all_to_all(r, "proto", 0, 0)
        if extra:
            zsums = sums
    half_g = vmem((rows, own), BF16)
    f, keep, give = call(
        functools.partial(grad_kernel, nb),
        "logit_grad",
        [
            hbm((npr, own_rows, dim), BF16),
            hbm((nb // 2, own, dim), F32),
            hbm((nb // 2, own, dim), BF16),
        ],
        [e, feats, b, sums, zsums, *pieces],
        halves
        + [lanes, lanes, half_g, half_g, vmem((rows, dim), F32), vmem((dim, rows), BF16)]
        + [vmem((nb // 2, own, dim), F32), vmem((nb // 2, own, dim), BF16)]
        + [pltpu.SemaphoreType.DMA((nb // 2, 2))],
        keep=(0, 2, 3, 4),
        raw=(1, *range(5, 5 + nb)),
        raw_out=(1, 2),
    )
    half = call(
        merge_kernel,
        "merge_cores",
        [hbm((own, dim), F32)] + [vmem((own, dim), BF16)] * (nb // 2 - 1),
        [keep, swap(give, 1)],
        keep=(1,),
    )
    got = [swap(x, 2 * k + 2) for k, x in enumerate(half[1:])]
    f, *got = lax.optimization_barrier((lax.all_to_all(f, "proto", 0, 0), *got))
    return call(
        final_kernel,
        "project_back",
        [jax.ShapeDtypeStruct((own_rows, dim), F32), jax.ShapeDtypeStruct((own, dim), F32)],
        [f, student_feats, student_protos, half[0], *got],
        keep=(0, *range(4, 3 + nb // 2)),
    )


def solution(mesh):
    nb, npr = mesh.shape["batch"], mesh.shape["proto"]
    in_specs = (
        P(("batch", "proto"), None),
        P(("batch", "proto"), None),
        P(("proto", "batch"), None),
        P(("proto", "batch"), None),
    )
    out_specs = (P(("batch", "proto"), None), P(("proto", "batch"), None))
    return jax.shard_map(
        functools.partial(shards, nb, npr),
        mesh=mesh,
        in_specs=in_specs,
        out_specs=out_specs,
        check_vma=False,
    )
```

```python
import functools

import jax
import jax.numpy as jnp
from jax import lax
from jax.experimental import pallas as pl
from jax.experimental.pallas import tpu as pltpu
from jax.sharding import PartitionSpec as P

ITERS = 3
LOG2E = 1.4426950408889634
teacher_temp = 0.07
student_temp = 0.1
epsilon = 1e-06

F32 = jnp.float32
BF16 = jnp.bfloat16
MIB = 2**20
VM = pl.BlockSpec(memory_space=pltpu.VMEM)
SM = pl.BlockSpec(memory_space=pltpu.SMEM)
NT = (((1,), (1,)), ((), ()))
NN = (((1,), (0,)), ((), ()))


def unit_rows(x):
    wide = x.astype(F32)
    scale = lax.rsqrt(jnp.sum(wide * wide, -1, keepdims=True) + epsilon)
    return (wide * scale, scale)


def project_back(grad, x):
    unit, scale = unit_rows(x)
    return (grad - unit * jnp.sum(unit * grad, -1, keepdims=True)) * scale


def fold(x):
    return x.reshape(-1, 8, x.shape[1]).sum(0)


def spread(row, out):
    for k in range(row.shape[1] // 128):
        part = row[:, k * 128 : (k + 1) * 128]
        out[k * 128 : (k + 1) * 128, :] = jnp.broadcast_to(part, (128, 128)).T


def gather_lanes(part, out):
    for k in range(part.shape[0] // 128):
        out[0:1, k * 128 : (k + 1) * 128] = part[k * 128 : (k + 1) * 128, :].T.sum(0, keepdims=True)


def unit_kernel(tf, sf, tp, sp, feats, protos):
    dim = tf.shape[1]
    for k, (x, y) in enumerate(((tf, tp), (sf, sp))):
        half = slice(k * dim, (k + 1) * dim)
        unit = unit_rows(x[...])[0].astype(BF16)
        for i in range(feats.shape[0]):
            feats[i, :, half] = unit
        protos[:, half] = unit_rows(y[...])[0].astype(BF16)


def load_half(half, feats, pieces, ft, pt, sem):
    dim = ft.shape[1]
    cols = pl.ds(half * dim, dim)
    first = pltpu.make_async_copy(feats.at[:, cols], ft, sem.at[len(pieces)])
    first.start()
    for r, piece in enumerate(pieces):
        pltpu.make_async_copy(piece.at[:, cols], pt.at[r], sem.at[r]).start()

    def wait_piece(r):
        pltpu.make_async_copy(pieces[0].at[:, cols], pt.at[r], sem.at[r]).wait()

    return first.wait, wait_piece


def exp_kernel(me, feats, *refs):
    pieces, (e, c, ft, pt, sem) = refs[:-5], refs[-5:]
    own = pt.shape[1]
    wait_feats, wait_piece = load_half(0, feats, pieces, ft, pt, sem)
    wait_feats()

    @pl.loop(0, len(pieces))
    def _(r):
        wait_piece(r)
        s = lax.dot_general(ft[...], pt[r], NT, preferred_element_type=F32)
        x = jnp.exp2(s * (LOG2E / teacher_temp))
        e[:, pl.ds(pl.multiple_of(r * own, own), own)] = x
        c[:, pl.ds(pl.multiple_of((me[0] ^ r) * own, own), own)] = fold(x).sum(0, keepdims=True)


def total_kernel(feats, *refs):
    pieces, (z, ft, pt, sem, part) = refs[:-5], refs[-5:]
    own = pt.shape[1]
    wait_feats, wait_piece = load_half(1, feats, pieces, ft, pt, sem)
    part[...] = jnp.zeros_like(part)
    wait_feats()

    @pl.loop(0, len(pieces))
    def _(r):
        wait_piece(r)
        s = lax.dot_general(ft[...], pt[r], NT, preferred_element_type=F32)
        x = jnp.exp2(s * (LOG2E / student_temp))
        acc = x[:, :128]
        for k in range(1, own // 128):
            acc += x[:, k * 128 : (k + 1) * 128]
        part[...] += acc

    gather_lanes(part, z)


def row_kernel(block, own, me, e, c0, c1, c2, c3, *refs):
    z, (r, b, part) = refs[:-3], refs[-3:]
    rows, cols = e.shape
    for k in range(cols // own):
        src = pl.ds(pl.multiple_of((me[0] ^ k) * own, own), own)
        b[:, k * own : (k + 1) * own] = 1.0 / (c0[:, src] + c1[:, src] + c2[:, src] + c3[:, src])

    @pl.loop(0, rows // block)
    def _(i):
        ii = pl.ds(pl.multiple_of(i * block, block), block)
        acc = jnp.zeros((block, 128), F32)
        for k in range(cols // 128):
            lanes = slice(k * 128, (k + 1) * 128)
            acc += e[ii, lanes] * b[:, lanes]
        part[ii, :] = acc

    gather_lanes(part, r.at[0])
    if z:
        r[0, 1:2, :] = z[0][...]
    for k in range(1, r.shape[0]):
        r[k] = r[0]


def col_kernel(block, width, own, me, e, sums, c, av):
    rows, cols = e.shape
    spread(1.0 / jnp.sum(sums[:, 0, :], 0, keepdims=True), av)
    for j in range(cols // width):

        def step(i, acc, j=j):
            ii = pl.ds(pl.multiple_of(i * block, block), block)
            w = av[ii, :]
            return tuple(
                acc[k] + fold(e[ii, j * width + k * 128 : j * width + (k + 1) * 128] * w)
                for k in range(width // 128)
            )

        zero = jnp.zeros((8, 128), F32)
        acc = lax.fori_loop(0, rows // block, step, (zero,) * (width // 128))
        for k in range(width // own):
            part = jnp.concatenate(acc[k * own // 128 : (k + 1) * own // 128], 1)
            to = (me[0] ^ (j * width // own + k)) * own
            c[:, pl.ds(pl.multiple_of(to, own), own)] = part.sum(0, keepdims=True)


def grad_kernel(count, e, feats, b, sums, zsums, *refs):
    pieces, refs = refs[:count], refs[count:]
    f, keep, give, ft, pt, sem, av, zv, g0, g1, acc, turned, kept, given, out_sem = refs
    own = pt.shape[1]
    wait_feats, wait_piece = load_half(1, feats, pieces, ft, pt, sem)
    spread((1.0 / student_temp) / jnp.sum(sums[:, 0, :], 0, keepdims=True), av)
    spread((1.0 / student_temp) / jnp.sum(zsums[:, 1, :], 0, keepdims=True), zv)
    acc[...] = jnp.zeros_like(acc)
    wait_feats()
    turned[...] = ft[...].T
    wide = lambda m: jnp.concatenate([m] * (own // 128), 1)

    def put(h, k):
        src, dst = ((kept, keep), (given, give))[k]
        return pltpu.make_async_copy(src.at[h], dst.at[h], out_sem.at[h, k])

    @pl.loop(0, count // 2)
    def _(h):
        new = []
        wait_piece(2 * h)
        wait_piece(2 * h + 1)
        for k, (g, out) in enumerate(((g0, kept), (g1, given))):
            cols = pl.ds(pl.multiple_of((2 * h + k) * own, own), own)
            sp = pt[2 * h + k]
            s = lax.dot_general(ft[...], sp, NT, preferred_element_type=F32)
            p = jnp.exp2(s * (LOG2E / student_temp))
            g[...] = (p * wide(zv[...]) - wide(av[...]) * (e[:, cols] * b[:, cols])).astype(BF16)
            out[h] = lax.dot_general(turned[...], g[...], NN, preferred_element_type=F32).T.astype(out.dtype)
            new.append(lax.dot_general(g[...], sp, NN, preferred_element_type=F32))
        acc[...] += new[0] + new[1]
        put(h, 0).start()
        put(h, 1).start()

    f[...] = acc[...].astype(BF16).reshape(f.shape)
    for h in range(count // 2):
        put(h, 0).wait()
        put(h, 1).wait()


def merge_kernel(keep, got, first, *rest):
    first[...] = keep[0] + got[0].astype(F32)
    for k, out in enumerate(rest):
        out[...] = (keep[k + 1] + got[k + 1].astype(F32)).astype(BF16)


def final_kernel(f, sf, sp, half, *refs):
    got, (f_out, p_out) = refs[:-2], refs[-2:]
    f_out[...] = project_back(jnp.sum(f[...].astype(F32), 0), sf[...])
    p = half[...]
    for x in got:
        p += x[...].astype(F32)
    p_out[...] = project_back(p, sp[...])


def call(kernel, name, out_shape, ops, scratch=(), limit=26, smem=0, keep=(), raw=(), raw_out=()):
    many = isinstance(out_shape, (list, tuple))
    ops = list(ops[:smem]) + [
        pltpu.with_memory_space_constraint(x, pltpu.VMEM if i in keep else pltpu.HBM)
        for i, x in enumerate(ops[smem:])
    ]
    whole = pl.BlockSpec(memory_space=pl.ANY)
    return pl.pallas_call(
        kernel,
        out_shape=out_shape,
        in_specs=[SM] * smem + [whole if i in raw else VM for i in range(len(ops) - smem)],
        out_specs=[whole if i in raw_out else VM for i in range(len(out_shape))] if many else VM,
        scratch_shapes=list(scratch),
        compiler_params=pltpu.CompilerParams(vmem_limit_bytes=limit * MIB),
        name=name,
    )(*ops)


def shards(nb, npr, teacher_feats, student_feats, teacher_protos, student_protos):
    swap = lambda x, k: lax.ppermute(x, "batch", [(i, i ^ k) for i in range(nb)])

    dim = teacher_feats.shape[1]
    own_rows, own = student_feats.shape[0], student_protos.shape[0]
    rows, cols = own_rows * npr, own * nb
    me = lax.axis_index("batch").astype(jnp.int32).reshape(1)
    hbm, vmem = pltpu.HBM, pltpu.VMEM

    feats, unit = call(
        unit_kernel,
        "unit_rows",
        [hbm((npr, own_rows, 2 * dim), BF16), hbm((own, 2 * dim), BF16)],
        [teacher_feats, student_feats, teacher_protos, student_protos],
    )
    pieces = [unit] + [None] * (nb - 1)
    for r in range(2, nb, 2):
        pieces[r] = swap(unit, r)
    feats = lax.all_to_all(feats, "proto", 0, 0).reshape(rows, 2 * dim)
    for r in range(0, nb, 2):
        pieces[r + 1] = swap(pieces[r], 1)

    lanes = vmem((rows, 128), F32)
    all_cols = vmem((1, cols), F32)
    halves = [vmem((rows, dim), BF16), vmem((nb, own, dim), BF16), pltpu.SemaphoreType.DMA((nb + 1,))]
    e, c = call(
        exp_kernel,
        "teacher_exp",
        [vmem((rows, cols), F32), all_cols],
        [me, feats, *pieces],
        halves,
        smem=1,
        raw=range(nb + 1),
    )
    for iteration in range(ITERS):
        if iteration:
            c = call(
                functools.partial(col_kernel, 128, 2048, own),
                "column_sums",
                all_cols,
                [me, e, sums],
                [lanes],
                smem=1,
                keep=(0, 1),
            )
        c = c + swap(c, 1)
        cs = [c] + [swap(c, k) for k in range(2, nb, 2)]
        if iteration == 1:
            z = call(
                total_kernel,
                "student_total",
                vmem((1, rows), F32),
                [feats, *pieces],
                halves + [lanes],
                limit=12,
                raw=range(nb + 1),
            )
        extra = [z] if iteration == 1 else []
        r, b = call(
            functools.partial(row_kernel, 128, own),
            "row_sums",
            [vmem((npr, 1 + len(extra), rows), F32), all_cols],
            [me, e, *cs, *extra],
            [lanes],
            smem=1,
            keep=(0, 1, 2, 3, 4, *([5] if extra else [])),
        )
        sums = lax.all_to_all(r, "proto", 0, 0)
        if extra:
            zsums = sums
    half_g = vmem((rows, own), BF16)
    f, keep, give = call(
        functools.partial(grad_kernel, nb),
        "logit_grad",
        [
            hbm((npr, own_rows, dim), BF16),
            hbm((nb // 2, own, dim), F32),
            hbm((nb // 2, own, dim), BF16),
        ],
        [e, feats, b, sums, zsums, *pieces],
        halves
        + [lanes, lanes, half_g, half_g, vmem((rows, dim), F32), vmem((dim, rows), BF16)]
        + [vmem((nb // 2, own, dim), F32), vmem((nb // 2, own, dim), BF16)]
        + [pltpu.SemaphoreType.DMA((nb // 2, 2))],
        keep=(0, 2, 3, 4),
        raw=(1, *range(5, 5 + nb)),
        raw_out=(1, 2),
    )
    half = call(
        merge_kernel,
        "merge_cores",
        [hbm((own, dim), F32)] + [vmem((own, dim), BF16)] * (nb // 2 - 1),
        [keep, swap(give, 1)],
        keep=(1,),
    )
    got = [swap(x, 2 * k + 2) for k, x in enumerate(half[1:])]
    f, *got = lax.optimization_barrier((lax.all_to_all(f, "proto", 0, 0), *got))
    return call(
        final_kernel,
        "project_back",
        [jax.ShapeDtypeStruct((own_rows, dim), F32), jax.ShapeDtypeStruct((own, dim), F32)],
        [f, student_feats, student_protos, half[0], *got],
        keep=(0, *range(4, 3 + nb // 2)),
    )


def solution(mesh):
    nb, npr = mesh.shape["batch"], mesh.shape["proto"]
    in_specs = (
        P(("batch", "proto"), None),
        P(("batch", "proto"), None),
        P(("proto", "batch"), None),
        P(("proto", "batch"), None),
    )
    out_specs = (P(("batch", "proto"), None), P(("proto", "batch"), None))
    return jax.shard_map(
        functools.partial(shards, nb, npr),
        mesh=mesh,
        in_specs=in_specs,
        out_specs=out_specs,
        check_vma=False,
    )
```

```python
import functools

import jax
import jax.numpy as jnp
from jax import lax
from jax.experimental import pallas as pl
from jax.experimental.pallas import tpu as pltpu
from jax.sharding import PartitionSpec as P

ITERS = 3
LOG2E = 1.4426950408889634
teacher_temp = 0.07
student_temp = 0.1
epsilon = 1e-06

F32 = jnp.float32
BF16 = jnp.bfloat16
MIB = 2**20
VM = pl.BlockSpec(memory_space=pltpu.VMEM)
SM = pl.BlockSpec(memory_space=pltpu.SMEM)
NT = (((1,), (1,)), ((), ()))
NN = (((1,), (0,)), ((), ()))


def unit_rows(x):
    wide = x.astype(F32)
    scale = lax.rsqrt(jnp.sum(wide * wide, -1, keepdims=True) + epsilon)
    return (wide * scale, scale)


def project_back(grad, x):
    unit, scale = unit_rows(x)
    return (grad - unit * jnp.sum(unit * grad, -1, keepdims=True)) * scale


def fold(x):
    return x.reshape(-1, 8, x.shape[1]).sum(0)


def spread(row, out):
    for k in range(row.shape[1] // 128):
        part = row[:, k * 128 : (k + 1) * 128]
        out[k * 128 : (k + 1) * 128, :] = jnp.broadcast_to(part, (128, 128)).T


def gather_lanes(part, out):
    for k in range(part.shape[0] // 128):
        out[0:1, k * 128 : (k + 1) * 128] = part[k * 128 : (k + 1) * 128, :].T.sum(0, keepdims=True)


def unit_kernel(tf, sf, tp, sp, feats, protos):
    dim = tf.shape[1]
    for k, (x, y) in enumerate(((tf, tp), (sf, sp))):
        half = slice(k * dim, (k + 1) * dim)
        unit = unit_rows(x[...])[0].astype(BF16)
        for i in range(feats.shape[0]):
            feats[i, :, half] = unit
        protos[:, half] = unit_rows(y[...])[0].astype(BF16)


def load_half(half, feats, pieces, ft, pt, sem):
    dim = ft.shape[1]
    cols = pl.ds(half * dim, dim)
    first = pltpu.make_async_copy(feats.at[:, cols], ft, sem.at[len(pieces)])
    first.start()
    for r, piece in enumerate(pieces):
        pltpu.make_async_copy(piece.at[:, cols], pt.at[r], sem.at[r]).start()

    def wait_piece(r):
        pltpu.make_async_copy(pieces[0].at[:, cols], pt.at[r], sem.at[r]).wait()

    return first.wait, wait_piece


def exp_kernel(me, feats, *refs):
    pieces, (e, c, ft, pt, sem) = refs[:-5], refs[-5:]
    own = pt.shape[1]
    wait_feats, wait_piece = load_half(0, feats, pieces, ft, pt, sem)
    wait_feats()

    @pl.loop(0, len(pieces))
    def _(r):
        wait_piece(r)
        s = lax.dot_general(ft[...], pt[r], NT, preferred_element_type=F32)
        x = jnp.exp2(s * (LOG2E / teacher_temp))
        e[:, pl.ds(pl.multiple_of(r * own, own), own)] = x
        c[:, pl.ds(pl.multiple_of((me[0] ^ r) * own, own), own)] = fold(x).sum(0, keepdims=True)


def total_kernel(feats, *refs):
    pieces, (z, ft, pt, sem, part) = refs[:-5], refs[-5:]
    own = pt.shape[1]
    wait_feats, wait_piece = load_half(1, feats, pieces, ft, pt, sem)
    part[...] = jnp.zeros_like(part)
    wait_feats()

    @pl.loop(0, len(pieces))
    def _(r):
        wait_piece(r)
        s = lax.dot_general(ft[...], pt[r], NT, preferred_element_type=F32)
        x = jnp.exp2(s * (LOG2E / student_temp))
        acc = x[:, :128]
        for k in range(1, own // 128):
            acc += x[:, k * 128 : (k + 1) * 128]
        part[...] += acc

    gather_lanes(part, z)


def row_kernel(block, own, me, e, c0, c1, c2, c3, *refs):
    z, (r, b, part) = refs[:-3], refs[-3:]
    rows, cols = e.shape
    for k in range(cols // own):
        src = pl.ds(pl.multiple_of((me[0] ^ k) * own, own), own)
        b[:, k * own : (k + 1) * own] = 1.0 / (c0[:, src] + c1[:, src] + c2[:, src] + c3[:, src])

    @pl.loop(0, rows // block)
    def _(i):
        ii = pl.ds(pl.multiple_of(i * block, block), block)
        acc = jnp.zeros((block, 128), F32)
        for k in range(cols // 128):
            lanes = slice(k * 128, (k + 1) * 128)
            acc += e[ii, lanes] * b[:, lanes]
        part[ii, :] = acc

    gather_lanes(part, r.at[0])
    if z:
        r[0, 1:2, :] = z[0][...]
    for k in range(1, r.shape[0]):
        r[k] = r[0]


def col_kernel(block, width, own, me, e, sums, c, av):
    rows, cols = e.shape
    spread(1.0 / jnp.sum(sums[:, 0, :], 0, keepdims=True), av)
    for j in range(cols // width):

        def step(i, acc, j=j):
            ii = pl.ds(pl.multiple_of(i * block, block), block)
            w = av[ii, :]
            return tuple(
                acc[k] + fold(e[ii, j * width + k * 128 : j * width + (k + 1) * 128] * w)
                for k in range(width // 128)
            )

        zero = jnp.zeros((8, 128), F32)
        acc = lax.fori_loop(0, rows // block, step, (zero,) * (width // 128))
        for k in range(width // own):
            part = jnp.concatenate(acc[k * own // 128 : (k + 1) * own // 128], 1)
            to = (me[0] ^ (j * width // own + k)) * own
            c[:, pl.ds(pl.multiple_of(to, own), own)] = part.sum(0, keepdims=True)


def grad_kernel(count, e, feats, b, sums, zsums, *refs):
    pieces, refs = refs[:count], refs[count:]
    f, keep, give, ft, pt, sem, av, zv, g0, g1, acc, turned, kept, given, out_sem = refs
    own = pt.shape[1]
    wait_feats, wait_piece = load_half(1, feats, pieces, ft, pt, sem)
    spread((1.0 / student_temp) / jnp.sum(sums[:, 0, :], 0, keepdims=True), av)
    spread((1.0 / student_temp) / jnp.sum(zsums[:, 1, :], 0, keepdims=True), zv)
    acc[...] = jnp.zeros_like(acc)
    wait_feats()
    turned[...] = ft[...].T
    wide = lambda m: jnp.concatenate([m] * (own // 128), 1)

    def put(h, k):
        src, dst = ((kept, keep), (given, give))[k]
        return pltpu.make_async_copy(src.at[h], dst.at[h], out_sem.at[h, k])

    @pl.loop(0, count // 2)
    def _(h):
        new = []
        wait_piece(2 * h)
        wait_piece(2 * h + 1)
        for k, (g, out) in enumerate(((g0, kept), (g1, given))):
            cols = pl.ds(pl.multiple_of((2 * h + k) * own, own), own)
            sp = pt[2 * h + k]
            s = lax.dot_general(ft[...], sp, NT, preferred_element_type=F32)
            p = jnp.exp2(s * (LOG2E / student_temp))
            g[...] = (p * wide(zv[...]) - wide(av[...]) * (e[:, cols] * b[:, cols])).astype(BF16)
            out[h] = lax.dot_general(turned[...], g[...], NN, preferred_element_type=F32).T.astype(out.dtype)
            new.append(lax.dot_general(g[...], sp, NN, preferred_element_type=F32))
        acc[...] += new[0] + new[1]
        put(h, 0).start()
        put(h, 1).start()

    f[...] = acc[...].astype(BF16).reshape(f.shape)
    for h in range(count // 2):
        put(h, 0).wait()
        put(h, 1).wait()


def merge_kernel(keep, got, first, *rest):
    first[...] = keep[0] + got[0].astype(F32)
    for k, out in enumerate(rest):
        out[...] = (keep[k + 1] + got[k + 1].astype(F32)).astype(BF16)


def final_kernel(f, sf, sp, half, *refs):
    got, (f_out, p_out) = refs[:-2], refs[-2:]
    f_out[...] = project_back(jnp.sum(f[...].astype(F32), 0), sf[...])
    p = half[...]
    for x in got:
        p += x[...].astype(F32)
    p_out[...] = project_back(p, sp[...])


def call(kernel, name, out_shape, ops, scratch=(), limit=26, smem=0, keep=(), raw=(), raw_out=()):
    many = isinstance(out_shape, (list, tuple))
    ops = list(ops[:smem]) + [
        pltpu.with_memory_space_constraint(x, pltpu.VMEM if i in keep else pltpu.HBM)
        for i, x in enumerate(ops[smem:])
    ]
    whole = pl.BlockSpec(memory_space=pl.ANY)
    return pl.pallas_call(
        kernel,
        out_shape=out_shape,
        in_specs=[SM] * smem + [whole if i in raw else VM for i in range(len(ops) - smem)],
        out_specs=[whole if i in raw_out else VM for i in range(len(out_shape))] if many else VM,
        scratch_shapes=list(scratch),
        compiler_params=pltpu.CompilerParams(vmem_limit_bytes=limit * MIB),
        name=name,
    )(*ops)


def shards(nb, npr, teacher_feats, student_feats, teacher_protos, student_protos):
    swap = lambda x, k: lax.ppermute(x, "batch", [(i, i ^ k) for i in range(nb)])

    dim = teacher_feats.shape[1]
    own_rows, own = student_feats.shape[0], student_protos.shape[0]
    rows, cols = own_rows * npr, own * nb
    me = lax.axis_index("batch").astype(jnp.int32).reshape(1)
    hbm, vmem = pltpu.HBM, pltpu.VMEM

    feats, unit = call(
        unit_kernel,
        "unit_rows",
        [hbm((npr, own_rows, 2 * dim), BF16), hbm((own, 2 * dim), BF16)],
        [teacher_feats, student_feats, teacher_protos, student_protos],
    )
    pieces = [unit] + [None] * (nb - 1)
    for r in range(2, nb, 2):
        pieces[r] = swap(unit, r)
    feats = lax.all_to_all(feats, "proto", 0, 0).reshape(rows, 2 * dim)
    for r in range(0, nb, 2):
        pieces[r + 1] = swap(pieces[r], 1)

    lanes = vmem((rows, 128), F32)
    all_cols = vmem((1, cols), F32)
    halves = [vmem((rows, dim), BF16), vmem((nb, own, dim), BF16), pltpu.SemaphoreType.DMA((nb + 1,))]
    e, c = call(
        exp_kernel,
        "teacher_exp",
        [vmem((rows, cols), F32), all_cols],
        [me, feats, *pieces],
        halves,
        smem=1,
        raw=range(nb + 1),
    )
    for iteration in range(ITERS):
        if iteration:
            c = call(
                functools.partial(col_kernel, 128, 2048, own),
                "column_sums",
                all_cols,
                [me, e, sums],
                [lanes],
                smem=1,
                keep=(0, 1),
            )
        c = c + swap(c, 1)
        cs = [c] + [swap(c, k) for k in range(2, nb, 2)]
        if iteration == 1:
            z = call(
                total_kernel,
                "student_total",
                vmem((1, rows), F32),
                [feats, *pieces],
                halves + [lanes],
                limit=12,
                raw=range(nb + 1),
            )
        extra = [z] if iteration == 1 else []
        r, b = call(
            functools.partial(row_kernel, 256, own),
            "row_sums",
            [vmem((npr, 1 + len(extra), rows), F32), all_cols],
            [me, e, *cs, *extra],
            [lanes],
            smem=1,
            keep=(0, 1, 2, 3, 4, *([5] if extra else [])),
        )
        sums = lax.all_to_all(r, "proto", 0, 0)
        if extra:
            zsums = sums
    half_g = vmem((rows, own), BF16)
    f, keep, give = call(
        functools.partial(grad_kernel, nb),
        "logit_grad",
        [
            hbm((npr, own_rows, dim), BF16),
            hbm((nb // 2, own, dim), F32),
            hbm((nb // 2, own, dim), BF16),
        ],
        [e, feats, b, sums, zsums, *pieces],
        halves
        + [lanes, lanes, half_g, half_g, vmem((rows, dim), F32), vmem((dim, rows), BF16)]
        + [vmem((nb // 2, own, dim), F32), vmem((nb // 2, own, dim), BF16)]
        + [pltpu.SemaphoreType.DMA((nb // 2, 2))],
        keep=(0, 2, 3, 4),
        raw=(1, *range(5, 5 + nb)),
        raw_out=(1, 2),
    )
    half = call(
        merge_kernel,
        "merge_cores",
        [hbm((own, dim), F32)] + [vmem((own, dim), BF16)] * (nb // 2 - 1),
        [keep, swap(give, 1)],
        keep=(1,),
    )
    got = [swap(x, 2 * k + 2) for k, x in enumerate(half[1:])]
    f, *got = lax.optimization_barrier((lax.all_to_all(f, "proto", 0, 0), *got))
    return call(
        final_kernel,
        "project_back",
        [jax.ShapeDtypeStruct((own_rows, dim), F32), jax.ShapeDtypeStruct((own, dim), F32)],
        [f, student_feats, student_protos, half[0], *got],
        keep=(0, *range(4, 3 + nb // 2)),
    )


def solution(mesh):
    nb, npr = mesh.shape["batch"], mesh.shape["proto"]
    in_specs = (
        P(("batch", "proto"), None),
        P(("batch", "proto"), None),
        P(("proto", "batch"), None),
        P(("proto", "batch"), None),
    )
    out_specs = (P(("batch", "proto"), None), P(("proto", "batch"), None))
    return jax.shard_map(
        functools.partial(shards, nb, npr),
        mesh=mesh,
        in_specs=in_specs,
        out_specs=out_specs,
        check_vma=False,
    )
```

```python
import functools

import jax
import jax.numpy as jnp
from jax import lax
from jax.experimental import pallas as pl
from jax.experimental.pallas import tpu as pltpu
from jax.sharding import PartitionSpec as P

ITERS = 3
LOG2E = 1.4426950408889634
teacher_temp = 0.07
student_temp = 0.1
epsilon = 1e-06

F32 = jnp.float32
BF16 = jnp.bfloat16
MIB = 2**20
VM = pl.BlockSpec(memory_space=pltpu.VMEM)
SM = pl.BlockSpec(memory_space=pltpu.SMEM)
NT = (((1,), (1,)), ((), ()))
NN = (((1,), (0,)), ((), ()))


def unit_rows(x):
    wide = x.astype(F32)
    scale = lax.rsqrt(jnp.sum(wide * wide, -1, keepdims=True) + epsilon)
    return (wide * scale, scale)


def project_back(grad, x):
    unit, scale = unit_rows(x)
    return (grad - unit * jnp.sum(unit * grad, -1, keepdims=True)) * scale


def fold(x):
    return x.reshape(-1, 8, x.shape[1]).sum(0)


def spread(row, out):
    for k in range(row.shape[1] // 128):
        part = row[:, k * 128 : (k + 1) * 128]
        out[k * 128 : (k + 1) * 128, :] = jnp.broadcast_to(part, (128, 128)).T


def gather_lanes(part, out):
    for k in range(part.shape[0] // 128):
        out[0:1, k * 128 : (k + 1) * 128] = part[k * 128 : (k + 1) * 128, :].T.sum(0, keepdims=True)


def unit_kernel(tf, sf, tp, sp, feats, protos):
    dim = tf.shape[1]
    for k, (x, y) in enumerate(((tf, tp), (sf, sp))):
        half = slice(k * dim, (k + 1) * dim)
        unit = unit_rows(x[...])[0].astype(BF16)
        for i in range(feats.shape[0]):
            feats[i, :, half] = unit
        protos[:, half] = unit_rows(y[...])[0].astype(BF16)


def load_half(half, feats, pieces, ft, pt, sem):
    dim = ft.shape[1]
    cols = pl.ds(half * dim, dim)
    first = pltpu.make_async_copy(feats.at[:, cols], ft, sem.at[len(pieces)])
    first.start()
    for r, piece in enumerate(pieces):
        pltpu.make_async_copy(piece.at[:, cols], pt.at[r], sem.at[r]).start()

    def wait_piece(r):
        pltpu.make_async_copy(pieces[0].at[:, cols], pt.at[r], sem.at[r]).wait()

    return first.wait, wait_piece


def exp_kernel(me, feats, *refs):
    pieces, (e, c, ft, pt, sem) = refs[:-5], refs[-5:]
    own = pt.shape[1]
    wait_feats, wait_piece = load_half(0, feats, pieces, ft, pt, sem)
    wait_feats()

    @pl.loop(0, len(pieces))
    def _(r):
        wait_piece(r)
        s = lax.dot_general(ft[...], pt[r], NT, preferred_element_type=F32)
        x = jnp.exp2(s * (LOG2E / teacher_temp))
        e[:, pl.ds(pl.multiple_of(r * own, own), own)] = x
        c[:, pl.ds(pl.multiple_of((me[0] ^ r) * own, own), own)] = fold(x).sum(0, keepdims=True)


def total_kernel(feats, *refs):
    pieces, (z, ft, pt, sem, part) = refs[:-5], refs[-5:]
    own = pt.shape[1]
    wait_feats, wait_piece = load_half(1, feats, pieces, ft, pt, sem)
    part[...] = jnp.zeros_like(part)
    wait_feats()

    @pl.loop(0, len(pieces))
    def _(r):
        wait_piece(r)
        s = lax.dot_general(ft[...], pt[r], NT, preferred_element_type=F32)
        x = jnp.exp2(s * (LOG2E / student_temp))
        acc = x[:, :128]
        for k in range(1, own // 128):
            acc += x[:, k * 128 : (k + 1) * 128]
        part[...] += acc

    gather_lanes(part, z)


def row_kernel(block, own, me, e, c0, c1, c2, c3, *refs):
    z, (r, b, part) = refs[:-3], refs[-3:]
    rows, cols = e.shape
    for k in range(cols // own):
        src = pl.ds(pl.multiple_of((me[0] ^ k) * own, own), own)
        b[:, k * own : (k + 1) * own] = 1.0 / (c0[:, src] + c1[:, src] + c2[:, src] + c3[:, src])

    @pl.loop(0, rows // block)
    def _(i):
        ii = pl.ds(pl.multiple_of(i * block, block), block)
        acc = jnp.zeros((block, 128), F32)
        for k in range(cols // 128):
            lanes = slice(k * 128, (k + 1) * 128)
            acc += e[ii, lanes] * b[:, lanes]
        part[ii, :] = acc

    gather_lanes(part, r.at[0])
    if z:
        r[0, 1:2, :] = z[0][...]
    for k in range(1, r.shape[0]):
        r[k] = r[0]


def col_kernel(block, width, own, me, e, sums, c, av):
    rows, cols = e.shape
    spread(1.0 / jnp.sum(sums[:, 0, :], 0, keepdims=True), av)
    for j in range(cols // width):

        def step(i, acc, j=j):
            ii = pl.ds(pl.multiple_of(i * block, block), block)
            w = av[ii, :]
            return tuple(
                acc[k] + fold(e[ii, j * width + k * 128 : j * width + (k + 1) * 128] * w)
                for k in range(width // 128)
            )

        zero = jnp.zeros((8, 128), F32)
        acc = lax.fori_loop(0, rows // block, step, (zero,) * (width // 128))
        for k in range(width // own):
            part = jnp.concatenate(acc[k * own // 128 : (k + 1) * own // 128], 1)
            to = (me[0] ^ (j * width // own + k)) * own
            c[:, pl.ds(pl.multiple_of(to, own), own)] = part.sum(0, keepdims=True)


def grad_kernel(count, e, feats, b, sums, zsums, *refs):
    pieces, refs = refs[:count], refs[count:]
    f, keep, give, ft, pt, sem, av, zv, g0, g1, acc, turned, kept, given, out_sem = refs
    own = pt.shape[1]
    wait_feats, wait_piece = load_half(1, feats, pieces, ft, pt, sem)
    spread((1.0 / student_temp) / jnp.sum(sums[:, 0, :], 0, keepdims=True), av)
    spread((1.0 / student_temp) / jnp.sum(zsums[:, 1, :], 0, keepdims=True), zv)
    acc[...] = jnp.zeros_like(acc)
    wait_feats()
    turned[...] = ft[...].T
    wide = lambda m: jnp.concatenate([m] * (own // 128), 1)

    def put(h, k):
        src, dst = ((kept, keep), (given, give))[k]
        return pltpu.make_async_copy(src.at[h], dst.at[h], out_sem.at[h, k])

    @pl.loop(0, count // 2)
    def _(h):
        new = []
        wait_piece(2 * h)
        wait_piece(2 * h + 1)
        for k, (g, out) in enumerate(((g0, kept), (g1, given))):
            cols = pl.ds(pl.multiple_of((2 * h + k) * own, own), own)
            sp = pt[2 * h + k]
            s = lax.dot_general(ft[...], sp, NT, preferred_element_type=F32)
            p = jnp.exp2(s * (LOG2E / student_temp))
            g[...] = (p * wide(zv[...]) - wide(av[...]) * (e[:, cols] * b[:, cols])).astype(BF16)
            out[h] = lax.dot_general(turned[...], g[...], NN, preferred_element_type=F32).T.astype(out.dtype)
            new.append(lax.dot_general(g[...], sp, NN, preferred_element_type=F32))
        acc[...] += new[0] + new[1]
        put(h, 0).start()
        put(h, 1).start()

    f[...] = acc[...].astype(BF16).reshape(f.shape)
    for h in range(count // 2):
        put(h, 0).wait()
        put(h, 1).wait()


def merge_kernel(keep, got, first, *rest):
    first[...] = keep[0] + got[0].astype(F32)
    for k, out in enumerate(rest):
        out[...] = (keep[k + 1] + got[k + 1].astype(F32)).astype(BF16)


def final_kernel(f, sf, sp, half, *refs):
    got, (f_out, p_out) = refs[:-2], refs[-2:]
    f_out[...] = project_back(jnp.sum(f[...].astype(F32), 0), sf[...])
    p = half[...]
    for x in got:
        p += x[...].astype(F32)
    p_out[...] = project_back(p, sp[...])


def call(kernel, name, out_shape, ops, scratch=(), limit=26, smem=0, keep=(), raw=(), raw_out=()):
    many = isinstance(out_shape, (list, tuple))
    ops = list(ops[:smem]) + [
        pltpu.with_memory_space_constraint(x, pltpu.VMEM if i in keep else pltpu.HBM)
        for i, x in enumerate(ops[smem:])
    ]
    whole = pl.BlockSpec(memory_space=pl.ANY)
    return pl.pallas_call(
        kernel,
        out_shape=out_shape,
        in_specs=[SM] * smem + [whole if i in raw else VM for i in range(len(ops) - smem)],
        out_specs=[whole if i in raw_out else VM for i in range(len(out_shape))] if many else VM,
        scratch_shapes=list(scratch),
        compiler_params=pltpu.CompilerParams(vmem_limit_bytes=limit * MIB),
        name=name,
    )(*ops)


def shards(nb, npr, teacher_feats, student_feats, teacher_protos, student_protos):
    swap = lambda x, k: lax.ppermute(x, "batch", [(i, i ^ k) for i in range(nb)])

    dim = teacher_feats.shape[1]
    own_rows, own = student_feats.shape[0], student_protos.shape[0]
    rows, cols = own_rows * npr, own * nb
    me = lax.axis_index("batch").astype(jnp.int32).reshape(1)
    hbm, vmem = pltpu.HBM, pltpu.VMEM

    feats, unit = call(
        unit_kernel,
        "unit_rows",
        [hbm((npr, own_rows, 2 * dim), BF16), hbm((own, 2 * dim), BF16)],
        [teacher_feats, student_feats, teacher_protos, student_protos],
    )
    pieces = [unit] + [None] * (nb - 1)
    for r in range(2, nb, 2):
        pieces[r] = swap(unit, r)
    feats = lax.all_to_all(feats, "proto", 0, 0).reshape(rows, 2 * dim)
    for r in range(0, nb, 2):
        pieces[r + 1] = swap(pieces[r], 1)

    lanes = vmem((rows, 128), F32)
    all_cols = vmem((1, cols), F32)
    halves = [vmem((rows, dim), BF16), vmem((nb, own, dim), BF16), pltpu.SemaphoreType.DMA((nb + 1,))]
    e, c = call(
        exp_kernel,
        "teacher_exp",
        [vmem((rows, cols), F32), all_cols],
        [me, feats, *pieces],
        halves,
        smem=1,
        raw=range(nb + 1),
    )
    for iteration in range(ITERS):
        if iteration:
            c = call(
                functools.partial(col_kernel, 256, 2048, own),
                "column_sums",
                all_cols,
                [me, e, sums],
                [lanes],
                smem=1,
                keep=(0, 1),
            )
        c = c + swap(c, 1)
        cs = [c] + [swap(c, k) for k in range(2, nb, 2)]
        if iteration == 1:
            z = call(
                total_kernel,
                "student_total",
                vmem((1, rows), F32),
                [feats, *pieces],
                halves + [lanes],
                limit=12,
                raw=range(nb + 1),
            )
        extra = [z] if iteration == 1 else []
        r, b = call(
            functools.partial(row_kernel, 256, own),
            "row_sums",
            [vmem((npr, 1 + len(extra), rows), F32), all_cols],
            [me, e, *cs, *extra],
            [lanes],
            smem=1,
            keep=(0, 1, 2, 3, 4, *([5] if extra else [])),
        )
        sums = lax.all_to_all(r, "proto", 0, 0)
        if extra:
            zsums = sums
    half_g = vmem((rows, own), BF16)
    f, keep, give = call(
        functools.partial(grad_kernel, nb),
        "logit_grad",
        [
            hbm((npr, own_rows, dim), BF16),
            hbm((nb // 2, own, dim), F32),
            hbm((nb // 2, own, dim), BF16),
        ],
        [e, feats, b, sums, zsums, *pieces],
        halves
        + [lanes, lanes, half_g, half_g, vmem((rows, dim), F32), vmem((dim, rows), BF16)]
        + [vmem((nb // 2, own, dim), F32), vmem((nb // 2, own, dim), BF16)]
        + [pltpu.SemaphoreType.DMA((nb // 2, 2))],
        keep=(0, 2, 3, 4),
        raw=(1, *range(5, 5 + nb)),
        raw_out=(1, 2),
    )
    half = call(
        merge_kernel,
        "merge_cores",
        [hbm((own, dim), F32)] + [vmem((own, dim), BF16)] * (nb // 2 - 1),
        [keep, swap(give, 1)],
        keep=(1,),
    )
    got = [swap(x, 2 * k + 2) for k, x in enumerate(half[1:])]
    f, *got = lax.optimization_barrier((lax.all_to_all(f, "proto", 0, 0), *got))
    return call(
        final_kernel,
        "project_back",
        [jax.ShapeDtypeStruct((own_rows, dim), F32), jax.ShapeDtypeStruct((own, dim), F32)],
        [f, student_feats, student_protos, half[0], *got],
        keep=(0, *range(4, 3 + nb // 2)),
    )


def solution(mesh):
    nb, npr = mesh.shape["batch"], mesh.shape["proto"]
    in_specs = (
        P(("batch", "proto"), None),
        P(("batch", "proto"), None),
        P(("proto", "batch"), None),
        P(("proto", "batch"), None),
    )
    out_specs = (P(("batch", "proto"), None), P(("proto", "batch"), None))
    return jax.shard_map(
        functools.partial(shards, nb, npr),
        mesh=mesh,
        in_specs=in_specs,
        out_specs=out_specs,
        check_vma=False,
    )
```
